256 devices in a mesh: row: 8 (over y, x_hi), col: 32 (over z, x_lo, core).
Axes of the slice: x: 4 (x_hi: 2, x_lo: 2; x = x_hi * 2 + x_lo), y: 4, z: 8, core: 2. Of those that a mesh axis runs over, the one named last changes fastest.
Arguments:
- activations: bfloat16 [256, 8192], P(None, 'col'), may hold values from -6 to 6
- out_grads: bfloat16 [256, 28672], P('col', 'row'), may hold values from -6 to 6
- input_basis: bfloat16 [8192, 8192], P('col', 'row'), may hold values from -0.0625 to 0.0625
- output_basis: bfloat16 [28672, 28672], P('row', 'col'), may hold values from -0.03125 to 0.03125
- eigenvalues: float32 [8192, 28672], P('row', 'col'), may hold values from 0.05 to 5
- query_inputs: bfloat16 [512, 8192], P(None, 'row'), may hold values from -0.015625 to 0.015625
- query_outgrads: bfloat16 [512, 28672], P(None, 'col'), may hold values from -0.0078125 to 0.0078125
Outputs:
- scores: float32 [32, 16], replicated
The draws below stay inside these ranges and needn't reach their ends.
All inputs are finite; a program needn't handle non-finite values.
Results may differ from the reference program's by a relative error of at most 0.0059.
Values may be sent and summed in bfloat16 or wider, within the bound.
A program may use at most 192 MiB of HBM per device.

```python
import math
import jax
import jax.numpy as jnp
from jax import lax

D_IN = 8192
D_OUT = 28672
SEQS = 16
TOK = 16
QUERIES = 32
QTOK = 16
ROWS = 256
QROWS = 512


def shard_levels(rng, dims, cuts, least, top_value):
    gain = 1.0
    for axis_at, parts in cuts:
        draws = jax.random.uniform(jax.random.fold_in(jax.random.fold_in(rng, 6), axis_at), (parts,), jnp.float32, least / len(cuts), top_value / len(cuts))
        gain = gain * jnp.repeat(jnp.exp(draws), dims[axis_at] // parts).reshape((-1,) + (1,) * (len(dims) - 1 - axis_at))
    return gain


def gaussian(key, dims, scale, limit, cuts=(), kind=jnp.bfloat16):
    gain = shard_levels(key, dims, cuts, -0.22, 0.18) if cuts else 1.0
    drawn = jax.random.normal(key, dims, jnp.float32) * scale * gain
    return jnp.minimum(jnp.maximum(drawn, -limit), limit).astype(kind)


def setup_inputs(seed: int = 0) -> dict:
    arg_keys = jax.random.split(jax.random.key(seed), 8)
    activations = gaussian(arg_keys[0], (ROWS, D_IN), 1.0, 6.0, ((1, 32),))
    out_grads = gaussian(arg_keys[1], (ROWS, D_OUT), 1.0, 6.0, ((0, 32), (1, 8)))
    input_basis = gaussian(arg_keys[2], (D_IN, D_IN), D_IN ** -0.5, 0.0625, ((0, 32), (1, 8)))
    output_basis = gaussian(arg_keys[3], (D_OUT, D_OUT), D_OUT ** -0.5, 0.03125, ((0, 8), (1, 32)))
    eigenvalues = jnp.clip(jnp.exp(math.log(5.0) - 4.6051702 * jax.random.uniform(arg_keys[4], (D_IN, D_OUT), jnp.float32) ** shard_levels(arg_keys[4], (D_IN, D_OUT), ((0, 8), (1, 32)), -0.2, 0.2)), 0.05, 5.0)
    query_inputs = gaussian(arg_keys[5], (QROWS, D_IN), (D_IN * TOK) ** -0.5, 0.015625, ((1, 8),))
    query_outgrads = gaussian(arg_keys[6], (QROWS, D_OUT), (D_OUT * QTOK) ** -0.5, 0.0078125, ((1, 32),))
    return dict(activations=activations, out_grads=out_grads, input_basis=input_basis, output_basis=output_basis, eigenvalues=eigenvalues, query_inputs=query_inputs, query_outgrads=query_outgrads)


damping = 0.05


def reference(activations, out_grads, input_basis, output_basis, eigenvalues, query_inputs, query_outgrads):
    rotated_in = jnp.dot(activations, input_basis, preferred_element_type=jnp.float32).astype(jnp.bfloat16)
    rotated_out = jnp.dot(out_grads, output_basis, preferred_element_type=jnp.float32).astype(jnp.bfloat16)
    seq_in = rotated_in.reshape(SEQS, TOK, D_IN).astype(jnp.float32)
    query_in = query_inputs.reshape(QUERIES, QTOK, D_IN).astype(jnp.float32)
    width = 128
    count = D_OUT // width

    def step(total, index):
        start = (index * width).astype(jnp.int32)
        seq_out = lax.dynamic_slice_in_dim(rotated_out, start, width, 1).reshape(SEQS, TOK, width).astype(jnp.float32)
        shifted = lax.dynamic_slice_in_dim(eigenvalues, start, width, 1) + damping
        grads = jnp.einsum('sti,stj->sij', seq_in, seq_out)
        scaled = lax.optimization_barrier((grads / shifted).astype(jnp.bfloat16)).astype(jnp.float32)
        query_out = lax.dynamic_slice_in_dim(query_outgrads, start, width, 1).reshape(QUERIES, QTOK, width).astype(jnp.float32)
        query_grad = jnp.einsum('qti,qtj->qij', query_in, query_out)
        query_grad = lax.optimization_barrier(query_grad.astype(jnp.bfloat16)).astype(jnp.float32)
        return total + jnp.einsum('qij,sij->qs', query_grad, scaled), None

    total, unused = lax.scan(step, jnp.zeros((QUERIES, SEQS), jnp.float32), jnp.arange(count, dtype=jnp.int32))
    return total
```

```python
import functools

import jax
import jax.numpy as jnp
from jax import lax
from jax.experimental import pallas as pl
from jax.experimental.pallas import tpu as pltpu
from jax.sharding import PartitionSpec as P

MESH = pl.DeviceIdType.MESH
F32, BF16, F8 = jnp.float32, jnp.bfloat16, jnp.float8_e4m3fn

D_I, D_J = 1024, 896
TOKENS, QUERIES, QTOK, SEQS = 256, 32, 16, 16
HALF = 1792
POOL = 14
DAMPING = 0.05
ORDER = (1, 7, 2, 6, 3, 5, 4)

RI_CORE, RI_X, RI_RS, RI_AG, RI_AGX, RI_AGC = 0, 1, 2, 9, 16, 17
OG_CORE, OG_Z, OG_X, OG_C = 18, 19, 26, 34
RO_RS, RO_AG = 50, 57
AR_C, AR_XY, AR_Z = 64, 65, 80
N_SEMS = 87


def power_scale(peak, top):
    scale = jnp.full_like(peak, 256.0 / top)
    for k in range(1, 15):
        scale = jnp.where(peak <= top * 0.25**k, 256.0 / top * 4.0**k, scale)
    return scale


def split8(x, top):
    scale = power_scale(jnp.max(jnp.abs(x), axis=(0, 1), keepdims=True), top)
    x = x * scale
    high = x.astype(F8).astype(F32)
    return high, x - high, scale


def kernel(
    act, ib, og, qi, qo, eig, ob, out,
    act_v, ib_v, qi_v, qo_v, eig_v, wt, qa, qb, scl, pool, ma, mb, pst,
    rip, r1, acc1, s2, r2, s3, s3f, r3, rig, riv,
    ogx, ogr, ogg, rop, ror, rog, rot, sc, ar_s, ar_r,
    lsem, ssem, rsem,
):
    row, col = lax.axis_index("row"), lax.axis_index("col")
    z, low = lax.div(col, 4), lax.rem(col, 4)
    xl, k = lax.div(low, 2), lax.rem(low, 2)
    core_peer = (row, col + 1 - 2 * k)
    x_col = z * 4 + lax.rem(low + 2, 4)
    x_peer = (row, x_col)

    def z_peer(d):
        return (row, lax.rem(z + d, 8) * 4 + low)

    def row_peer(d):
        return (lax.rem(row + d, 8), col)

    xy = [(d, e) for d in range(8) for e in range(2) if d or e]

    def xy_peer(d, e):
        return (lax.rem(row + d, 8), x_col if e else col)

    barrier = pltpu.get_barrier_semaphore()
    peers = [core_peer] + [z_peer(d) for d in range(1, 8)] + [xy_peer(d, e) for d, e in xy]
    for p in peers:
        pl.semaphore_signal(barrier, inc=1, device_id=p, device_id_type=MESH)

    started = []

    def send(src, dst, sem, peer):
        c = pltpu.make_async_remote_copy(
            src_ref=src, dst_ref=dst, send_sem=ssem.at[sem], recv_sem=rsem.at[sem],
            device_id=peer, device_id_type=MESH,
        )
        c.start()
        started.append(c)
        return c

    def fetch(src, dst, sem):
        c = pltpu.make_async_copy(src, dst, lsem.at[sem])
        c.start()
        return c

    ob_v = pool.at[pl.ds(0, 2 * HALF), pl.ds(0, D_J)]
    get_act = fetch(act, act_v, 0)
    get_ib = fetch(ib, ib_v, 1)
    get_eig = [fetch(eig.at[pl.ds(256 * c, 256)], eig_v.at[c % 2], 2 + c) for c in range(2)]
    get_qi = fetch(qi, qi_v, 6)
    get_qo = fetch(qo, qo_v, 7)

    own_og = og[...].astype(F32)
    ogx[0] = own_og[:, :HALF]
    ogx[1] = own_og[:, HALF:]

    get_act.wait()
    get_ib.wait()
    part = jnp.dot(act_v[...], ib_v[...], preferred_element_type=F32)
    rip[...] = part

    for c in range(4):
        get_eig[c].wait()
        wt[:, pl.ds(256 * c, 256)] = 1.0 / (eig_v[c % 2].T + DAMPING)
        if c < 2:
            get_eig.append(fetch(eig.at[pl.ds(256 * (c + 2), 256)], eig_v.at[c % 2], 4 + c))
    get_ob = fetch(ob, ob_v, 8)
    get_qi.wait()
    get_qo.wait()

    pl.semaphore_wait(barrier, len(peers))

    ri_c = send(
        rip.at[pl.ds(pl.multiple_of(128 - 128 * k, 128), 128), :], r1, RI_CORE, core_peer
    )
    og_c = send(ogx.at[1 - k], ogr, OG_CORE, core_peer)

    def prepare(pair, carry):
        sides = []
        for e in range(2):
            q = 2 * pair + e
            rows = pl.ds(pl.multiple_of(q * QTOK, QTOK), QTOK)
            high, rest, a = split8(qi_v[rows, :].astype(F32), 2.0**-6)
            used = jnp.concatenate([high, rest, high, rest], axis=0)
            none = jnp.zeros_like(used)
            qb[q] = jnp.concatenate([none, used] if e else [used, none], axis=0).astype(F8)
            high, rest, b = split8(qo_v[rows, :].astype(F32), 2.0**-7)
            sides.append(jnp.concatenate([high, high, rest, rest], axis=0))
            scl[pl.ds(q, 1), :] = jnp.broadcast_to(1.0 / (a * b), (1, TOKENS))
        both = jnp.concatenate(sides, axis=0).astype(BF16)
        qa[pair] = both.T.astype(F32).astype(F8)
        return carry

    def weighted(q):
        g = jnp.dot(qa[lax.div(q, 2)], qb[q], preferred_element_type=F32)
        return (g * wt[...]).astype(BF16)

    def fill(slot, carry):
        rows = pl.ds(pl.multiple_of(slot * D_J, D_J), D_J)
        pool[rows, :] = weighted(slot)
        return carry

    lax.fori_loop(0, 4, prepare, 0)

    ri_c.wait_recv()
    acc = rip[pl.ds(pl.multiple_of(128 * k, 128), 128), :] + r1[...]
    acc1[...] = acc
    s2[0] = acc[:64].astype(BF16)
    s2[1] = acc[64:].astype(BF16)
    ri_x = send(s2.at[1 - xl], r2, RI_X, x_peer)

    og_c.wait_recv()
    mine = ogx[k]
    other = ogr[...]
    first = jnp.where(k == 0, mine, other)
    second = jnp.where(k == 0, other, mine)
    own_seq = 2 * z + xl
    ogg[k, own_seq] = jnp.concatenate([first, second], axis=0).astype(BF16)

    def og_send(n):
        d = ORDER[n]
        block = ogg.at[k, own_seq]
        return send(block, block, OG_Z + n, z_peer(d))

    og_z = [og_send(n) for n in range(4)]
    og_x, og_f = [], []

    def og_forward(n):
        if n:
            og_z[n - 1].wait_recv()
            d = ORDER[n - 1]
            block = ogg.at[k, 2 * lax.rem(z + 8 - d, 8) + xl]
        else:
            block = ogg.at[k, own_seq]
        og_x.append(send(block, block, OG_X + n, x_peer))
        og_f.append(send(block, block, OG_C + n, core_peer))

    def og_forward_x(n):
        og_x[n].wait_recv()
        d = ORDER[n - 1] if n else 0
        block = ogg.at[k, 2 * lax.rem(z + 8 - d, 8) + 1 - xl]
        og_f.append(send(block, block, OG_C + 8 + n, core_peer))

    og_forward(0)
    lax.fori_loop(4, 16, prepare, 0)

    ri_x.wait_recv()
    acc = acc1[pl.ds(pl.multiple_of(64 * xl, 64), 64), :] + r2[...].astype(F32)
    for c in range(8):
        piece = acc[16 * (c % 4) : 16 * (c % 4) + 16, 512 * (c // 4) : 512 * (c // 4) + 512]
        s3f[c] = piece
        s3[c] = piece.astype(BF16)
    ri_rs = [send(s3.at[lax.rem(z + d, 8)], r3.at[d], RI_RS + d - 1, z_peer(d)) for d in range(1, 8)]
    og_z += [og_send(n) for n in range(4, 7)]

    lax.fori_loop(4, 9, fill, 0)
    for n in range(1, 5):
        og_forward(n)

    for c in ri_rs:
        c.wait_recv()
    total = s3f[z]
    for d in range(1, 8):
        total = total + r3[d].astype(F32)
    rig[k, xl, z] = total.astype(BF16)
    block = rig.at[k, xl, z]
    ri_ag = [send(block, block, RI_AG + d - 1, z_peer(d)) for d in range(1, 8)]

    lax.fori_loop(9, POOL, fill, 0)
    for n in range(5, 8):
        og_forward(n)

    for c in ri_ag:
        c.wait_recv()
    ri_agx = send(rig.at[k, xl], rig.at[k, xl], RI_AGX, x_peer)
    for n in range(8):
        og_forward_x(n)
    ri_agx.wait_recv()
    ri_agc = send(rig.at[k], rig.at[k], RI_AGC, core_peer)

    get_ob.wait()
    for c in og_f:
        c.wait_recv()
    part = jnp.dot(
        ogg[0].reshape(TOKENS, HALF), pool[pl.ds(0, HALF), pl.ds(0, D_J)], preferred_element_type=F32
    ) + jnp.dot(
        ogg[1].reshape(TOKENS, HALF), pool[pl.ds(HALF, HALF), pl.ds(0, D_J)], preferred_element_type=F32
    )
    rop[...] = part
    ro_rs = [
        send(
            rop.at[pl.ds(pl.multiple_of(32 * lax.rem(row + d, 8), 32), 32), :],
            ror.at[d - 1], RO_RS + d - 1, row_peer(d),
        )
        for d in range(1, 8)
    ]
    lax.fori_loop(0, 4, fill, 0)

    ri_agc.wait_recv()
    for a in range(2):
        for b in range(2):
            for c in range(8):
                at = 128 * a + 64 * b + 16 * (c % 4)
                riv[at : at + 16, 512 * (c // 4) : 512 * (c // 4) + 512] = rig[a, b, c]

    def contract(m):
        return lax.dot_general(m, riv[...], (((1,), (1,)), ((), ())), preferred_element_type=F32)

    def early(n, carry):
        rows = pl.ds(pl.multiple_of(n * 2 * D_J, 2 * D_J), 2 * D_J)
        pst[rows, :] = contract(pool[rows, :]).astype(BF16)
        return carry

    lax.fori_loop(0, POOL // 4, early, 0)

    for c in ro_rs:
        c.wait_recv()
    total = rop[pl.ds(pl.multiple_of(32 * row, 32), 32), :]
    for d in range(1, 8):
        total = total + ror[d - 1]
    rog[row] = total.astype(BF16)
    block = rog.at[row]
    ro_ag = [send(block, block, RO_AG + d - 1, row_peer(d)) for d in range(1, 8)]

    lax.fori_loop(POOL // 4, POOL // 2, early, 0)
    ma[...] = weighted(POOL)
    for c in ro_ag:
        c.wait_recv()
    rot[...] = rog[...].reshape(TOKENS, D_J).T.astype(F32)

    def score(q, p):
        sc[pl.ds(q, 1), :] = jnp.sum(p * rot[...], axis=0, keepdims=True)

    late = QUERIES - POOL

    def finish(n, carry):
        for u, (src, dst) in enumerate(((ma, mb), (mb, ma))):
            q = POOL + 2 * n + u
            score(q, contract(src[...]))
            dst[...] = weighted(jnp.minimum(q + 1, QUERIES - 1))
            old = jnp.minimum(2 * n + u, POOL - 1)
            rows = pl.ds(pl.multiple_of(old * D_J, D_J), D_J)
            score(old, pst[rows, :].astype(F32))
        return carry

    lax.fori_loop(0, late // 2, finish, 0)

    parts = sc[...] * scl[...]
    token = lax.broadcasted_iota(jnp.int32, (TOKENS, 128), 0)
    lane = lax.broadcasted_iota(jnp.int32, (TOKENS, 128), 1)
    packed = jnp.zeros((8, 128), F32)
    for b in range(4):
        pick = jnp.where(lane == 16 * b + lax.div(token, 16), 1.0, 0.0)
        packed = packed + jnp.dot(
            parts[8 * b : 8 * b + 8], pick, precision=lax.Precision.HIGHEST, preferred_element_type=F32
        )
    ar_s[0] = packed
    c = send(ar_s.at[0], ar_r.at[0], AR_C, core_peer)
    c.wait_recv()
    packed = packed + ar_r[0]
    ar_s[1] = packed
    hops = [send(ar_s.at[1], ar_r.at[1 + n], AR_XY + n, xy_peer(d, e)) for n, (d, e) in enumerate(xy)]
    for c in hops:
        c.wait_recv()
    packed = packed + sum(ar_r[1 + n] for n in range(15))
    ar_s[2] = packed
    hops = [send(ar_s.at[2], ar_r.at[16 + d - 1], AR_Z + d - 1, z_peer(d)) for d in range(1, 8)]
    for c in hops:
        c.wait_recv()
    packed = packed + sum(ar_r[16 + n] for n in range(7))
    for b in range(4):
        out[8 * b : 8 * b + 8, :] = packed[:, 16 * b : 16 * b + 16]

    for c in started:
        c.wait_send()


def per_device(
    activations, out_grads, input_basis, output_basis, eigenvalues, query_inputs, query_outgrads
):
    any_, vmem = pl.BlockSpec(memory_space=pl.ANY), pl.BlockSpec(memory_space=pltpu.VMEM)
    scratch = [
        ((256, 256), BF16), ((256, D_I), BF16), ((512, D_I), BF16), ((512, D_J), BF16),
        ((2, 256, D_J), F32), ((D_J, D_I), F32), ((16, D_J, 128), F8), ((QUERIES, 128, D_I), F8),
        ((QUERIES, TOKENS), F32), ((POOL * D_J, D_I), BF16), ((D_J, D_I), BF16), ((D_J, D_I), BF16),
        ((POOL * D_J, TOKENS), BF16),
        ((256, D_I), F32), ((128, D_I), F32), ((128, D_I), F32),
        ((2, 64, D_I), BF16), ((64, D_I), BF16), ((8, 16, 512), BF16), ((8, 16, 512), F32),
        ((8, 16, 512), BF16), ((2, 2, 8, 16, 512), BF16), ((256, D_I), BF16),
        ((2, 8, HALF), F32), ((8, HALF), F32), ((2, 16, 16, HALF), BF16),
        ((256, D_J), F32), ((7, 32, D_J), F32), ((8, 32, D_J), BF16),
        ((D_J, TOKENS), F32), ((QUERIES, TOKENS), F32), ((3, 8, 128), F32), ((23, 8, 128), F32),
    ]
    return pl.pallas_call(
        kernel,
        out_shape=jax.ShapeDtypeStruct((QUERIES, SEQS), F32),
        in_specs=[any_, any_, vmem, any_, any_, any_, any_],
        out_specs=vmem,
        scratch_shapes=[pltpu.VMEM(s, t) for s, t in scratch]
        + [pltpu.SemaphoreType.DMA((9,)), pltpu.SemaphoreType.DMA((N_SEMS,)), pltpu.SemaphoreType.DMA((N_SEMS,))],
        compiler_params=pltpu.CompilerParams(
            collective_id=0, has_side_effects=True, vmem_limit_bytes=63 * 2**20
        ),
        name="influence",
    )(activations, input_basis, out_grads, query_inputs, query_outgrads, eigenvalues, output_basis)


def solution(mesh):
    in_specs = (
        P(None, "col"),
        P("col", "row"),
        P("col", "row"),
        P("row", "col"),
        P("row", "col"),
        P(None, "row"),
        P(None, "col"),
    )
    return jax.shard_map(
        per_device, mesh=mesh, in_specs=in_specs, out_specs=P(), check_vma=False
    )
```

```python
import functools

import jax
import jax.numpy as jnp
from jax import lax
from jax.experimental import pallas as pl
from jax.experimental.pallas import tpu as pltpu
from jax.sharding import PartitionSpec as P

MESH = pl.DeviceIdType.MESH
F32, BF16 = jnp.float32, jnp.bfloat16

D_I, D_J = 1024, 896
TOKENS, QUERIES, QTOK, SEQS = 256, 32, 16, 16
HALF = 1792
POOL = 16
PARTS = 2
WIDE = D_I // PARTS
DAMPING = 0.05
ORDER = (0, 1, 7, 2, 6, 3, 5, 4)

RI_CORE = 0
RI_X = RI_CORE + PARTS
RI_RS = RI_X + PARTS
RI_AG = RI_RS + 7 * PARTS
RI_AGX = RI_AG + 7 * PARTS
RI_AGC = RI_AGX + PARTS
OG_CORE = RI_AGC + PARTS
OG_Z = OG_CORE + 1
OG_X = OG_Z + 8
OG_C = OG_X + 8
RO_RS = OG_C + 16
RO_AG = RO_RS + 14
AR_C = RO_AG + 14
AR_XY = AR_C + 1
AR_Z = AR_XY + 15
N_SEMS = AR_Z + 7


def kernel(
    act, ib, og, qi, qo, eig, ob, out, spilled,
    act_v, ib_v, qi_v, qo_v, eig_v, wt, qa, pool, pst,
    rip, r1, acc1, s2, r2, s3, s3f, r3, rig, riv,
    ogx, ogr, ogg, rop, ros, ror, rog, rot, sc, ar_s, ar_r,
    lsem, osem, isem, ssem, rsem,
):
    row, col = lax.axis_index("row"), lax.axis_index("col")
    z, low = lax.div(col, 4), lax.rem(col, 4)
    xl, k = lax.div(low, 2), lax.rem(low, 2)
    core_peer = (row, col + 1 - 2 * k)
    x_col = z * 4 + lax.rem(low + 2, 4)
    x_peer = (row, x_col)

    def z_peer(d):
        return (row, lax.rem(z + d, 8) * 4 + low)

    def row_peer(d):
        return (lax.rem(row + d, 8), col)

    xy = [(d, e) for d in range(8) for e in range(2) if d or e]

    def xy_peer(d, e):
        return (lax.rem(row + d, 8), x_col if e else col)

    barrier = pltpu.get_barrier_semaphore()
    peers = [z_peer(d) for d in ORDER[:0:-1]] + [xy_peer(d, e) for d, e in xy] + [core_peer]
    for p in peers:
        pl.semaphore_signal(barrier, inc=1, device_id=p, device_id_type=MESH)

    started = []

    def send(src, dst, sem, peer):
        c = pltpu.make_async_remote_copy(
            src_ref=src, dst_ref=dst, send_sem=ssem.at[sem], recv_sem=rsem.at[sem],
            device_id=peer, device_id_type=MESH,
        )
        c.start()
        started.append(c)
        return c

    def fetch(src, dst, sem):
        c = pltpu.make_async_copy(src, dst, lsem.at[sem])
        c.start()
        return c

    ob_v = pool.at[pl.ds(0, 2 * HALF), pl.ds(0, D_J)]
    get_act = fetch(act, act_v, 0)
    get_ib = fetch(ib, ib_v, 1)
    get_eig = [fetch(eig.at[pl.ds(256 * c, 256)], eig_v.at[c % 2], 2 + c) for c in range(2)]
    get_qi = fetch(qi, qi_v, 6)
    get_qo = fetch(qo, qo_v, 7)

    own_og = og[...].astype(F32)
    ogx[0] = own_og[:, :HALF]
    ogx[1] = own_og[:, HALF:]

    get_act.wait()
    get_ib.wait()
    rip[...] = jnp.dot(act_v[...], ib_v[...], preferred_element_type=F32)

    pl.semaphore_wait(barrier, len(peers))

    def lanes(h):
        return pl.ds(WIDE * h, WIDE)

    og_c = send(ogx.at[1 - k], ogr, OG_CORE, core_peer)
    other_half = pl.ds(pl.multiple_of(128 - 128 * k, 128), 128)
    ri_c = [
        send(rip.at[other_half, lanes(h)], r1.at[:, lanes(h)], RI_CORE + h, core_peer)
        for h in range(PARTS)
    ]

    def slot_rows(slot, count=1):
        return pl.ds(pl.multiple_of(slot * D_J, D_J), count * D_J)

    def weighted(q, slot):
        group = lax.div(q, 8)
        tokens = qi_v[pl.ds(pl.multiple_of(group * 128, 128), 128), :]
        token = lax.broadcasted_iota(jnp.int32, tokens.shape, 0)
        own = jnp.where(lax.div(token, QTOK) == lax.rem(q, 8), tokens, jnp.zeros_like(tokens))
        for half in range(2):
            at = pl.ds(448 * half, 448)
            g = jnp.dot(qa[group, at, :], own, preferred_element_type=F32)
            rows = pl.ds(pl.multiple_of(slot * D_J + 448 * half, 448), 448)
            pool[rows, :] = (g.astype(BF16).astype(F32) * wt[at, :]).astype(BF16)

    def spill_copy(n, slot):
        return pltpu.make_async_copy(pool.at[slot_rows(slot), :], spilled.at[slot_rows(n), :], osem.at[n])

    def spill(n, carry):
        weighted(POOL + n, 4 + n)
        spill_copy(n, 4 + n).start()
        return carry

    def spill_last(n, carry):
        spill_copy(n - 12, n - 8).wait()
        weighted(POOL + n, n - 8)
        spill_copy(n, n - 8).start()
        return carry

    def fill_after_last(slot, carry):
        spill_copy(slot + 8, slot).wait()
        weighted(slot, slot)
        return carry

    def fill_after(slot, carry):
        spill_copy(slot - 4, slot).wait()
        weighted(slot, slot)
        return carry

    def fill(slot, carry):
        weighted(slot, slot)
        return carry

    for h in range(PARTS):
        ri_c[h].wait_recv()
    acc = rip[pl.ds(pl.multiple_of(128 * k, 128), 128), :] + r1[...]
    acc1[...] = acc
    s2[0] = acc[:64].astype(BF16)
    s2[1] = acc[64:].astype(BF16)
    ri_x = [
        send(s2.at[1 - xl, :, lanes(h)], r2.at[:, lanes(h)], RI_X + h, x_peer) for h in range(PARTS)
    ]

    og_c.wait_recv()
    mine = ogx[k]
    other = ogr[...]
    first = jnp.where(k == 0, mine, other)
    second = jnp.where(k == 0, other, mine)
    ogg[k, 0, xl] = jnp.concatenate([first, second], axis=0).astype(BF16)

    def og_send(n):
        return send(ogg.at[k, 0, xl], ogg.at[k, n, xl], OG_Z + n, z_peer(ORDER[n]))

    def og_pass(n, to, d):
        block = ogg.at[k, n, xl]
        og_z[to] = send(block, ogg.at[k, to, xl], OG_Z + to, z_peer(d))

    og_z = {n: og_send(n) for n in range(1, 5)}
    og_x, og_f = {}, {}

    def og_forward(n):
        if n:
            og_z[n].wait_recv()
        block = ogg.at[k, n, xl]
        if n not in (1, 2):
            og_x[n] = send(block, block, OG_X + n, x_peer)
        og_f[2 * n] = send(block, block, OG_C + 2 * n, core_peer)

    def og_forward_x(n):
        og_x[n].wait_recv()
        block = ogg.at[k, n, 1 - xl]
        og_f[2 * n + 1] = send(block, block, OG_C + 2 * n + 1, core_peer)
        if n == 0:
            for to, d in ((1, 1), (2, 7)):
                og_x[to] = send(block, ogg.at[k, to, 1 - xl], OG_X + to, z_peer(d))

    og_forward(0)
    for c in range(4):
        get_eig[c].wait()
        wt[:, pl.ds(256 * c, 256)] = 1.0 / (eig_v[c % 2].T + DAMPING)
        if c < 2:
            get_eig.append(fetch(eig.at[pl.ds(256 * (c + 2), 256)], eig_v.at[c % 2], 4 + c))
    get_ob = fetch(ob, ob_v, 8)
    get_qi.wait()
    get_qo.wait()
    for group in range(4):
        qa[group] = qo_v[128 * group : 128 * group + 128, :].T

    lax.fori_loop(0, 3, spill, 0)

    ri_rs = []
    for h in range(PARTS):
        ri_x[h].wait_recv()
        acc = acc1[pl.ds(pl.multiple_of(64 * xl, 64), 64), lanes(h)] + r2[:, lanes(h)].astype(F32)
        for c in range(8):
            at = WIDE // 2 * (c // 4)
            piece = acc[16 * (c % 4) : 16 * (c % 4) + 16, at : at + WIDE // 2]
            s3f[h, c] = piece
            s3[h, c] = piece.astype(BF16)
        ri_rs.append(
            [
                send(s3.at[h, lax.rem(z + d, 8)], r3.at[h, d], RI_RS + 7 * h + d - 1, z_peer(d))
                for d in ORDER[:0:-1]
            ]
        )
    og_forward_x(0)
    lax.fori_loop(3, 6, spill, 0)
    for n in range(3, 5):
        og_forward(n)
    og_pass(3, 5, 1)
    og_pass(4, 6, 7)
    og_pass(3, 7, 2)
    for n in range(1, 3):
        og_forward(n)

    lax.fori_loop(6, 12, spill, 0, unroll=2)
    for n in range(1, 4):
        og_forward_x(n)
    lax.fori_loop(12, 16, spill_last, 0, unroll=2)

    ri_ag = []
    for h in range(PARTS):
        for c in ri_rs[h]:
            c.wait_recv()
        total = s3f[h, z]
        for d in range(1, 8):
            total = total + r3[h, d].astype(F32)
        rig[k, h, xl, z] = total.astype(BF16)
        block = rig.at[k, h, xl, z]
        ri_ag.append([send(block, block, RI_AG + 7 * h + d - 1, z_peer(d)) for d in ORDER[:0:-1]])

    lax.fori_loop(8, 10, fill_after, 0, unroll=2)
    for n in range(5, 8):
        og_forward(n)
    og_forward_x(4)
    lax.fori_loop(10, 14, fill_after, 0, unroll=2)

    def ro_start(c):
        for n in range(8 * c, 8 * c + 8):
            og_f[n].wait_recv()
        tokens = [ogg[a, 4 * c : 4 * c + 4].reshape(128, HALF) for a in range(2)]
        part = jnp.dot(tokens[0], pool[pl.ds(0, HALF), pl.ds(0, D_J)], preferred_element_type=F32)
        part = part + jnp.dot(
            tokens[1], pool[pl.ds(HALF, HALF), pl.ds(0, D_J)], preferred_element_type=F32
        )
        rop[c] = part.reshape(8, 16, D_J)
        ros[c] = part.reshape(8, 16, D_J).astype(BF16)
        return [
            send(ros.at[c, lax.rem(row + d, 8)], ror.at[c, d - 1], RO_RS + 7 * c + d - 1, row_peer(d))
            for d in range(1, 8)
        ]

    def ro_sum(c):
        for f in ro_rs[c]:
            f.wait_recv()
        total = rop[c, row]
        for d in range(1, 8):
            total = total + ror[c, d - 1].astype(F32)
        n = 4 * c + lax.div(row, 2)
        far = lax.div(n + 1, 2)
        source = lax.rem(jnp.where(lax.rem(n, 2) == 1, z + 8 - far, z + far), 8)
        seq = 2 * source + lax.rem(row, 2)
        rog[seq] = total.astype(BF16)
        block = rog.at[seq]
        return [send(block, block, RO_AG + 7 * c + d - 1, row_peer(d)) for d in range(1, 8)]

    get_ob.wait()
    ro_rs = [ro_start(0)]
    lax.fori_loop(14, 16, fill_after, 0, unroll=2)
    lax.fori_loop(4, 6, fill_after_last, 0, unroll=2)

    ri_agx = []
    for h in range(PARTS):
        for c in ri_ag[h]:
            c.wait_recv()
        block = rig.at[k, h, xl]
        ri_agx.append(send(block, block, RI_AGX + h, x_peer))

    lax.fori_loop(6, 8, fill_after_last, 0, unroll=2)
    for n in range(5, 8):
        og_forward_x(n)
    ri_agc = []
    for h in range(PARTS):
        ri_agx[h].wait_recv()
        ri_agc.append(send(rig.at[k, h], rig.at[k, h], RI_AGC + h, core_peer))

    ro_rs.append(ro_start(1))
    lax.fori_loop(0, 4, fill, 0, unroll=2)

    for h in range(PARTS):
        ri_agc[h].wait_recv()
        for a in range(2):
            for b in range(2):
                for c in range(8):
                    at = 128 * a + 64 * b + 16 * (c % 4)
                    lane = WIDE * h + WIDE // 2 * (c // 4)
                    riv[at : at + 16, lane : lane + WIDE // 2] = rig[a, h, b, c]

    def fetch_four(n):
        rows = slot_rows(4 * n, 4)
        return pltpu.make_async_copy(spilled.at[rows, :], pool.at[rows, :], isem.at[n])

    def contract(n, to):
        for part in range(4):
            pst[slot_rows(4 * to + part), :] = lax.dot_general(
                pool[slot_rows(4 * n + part), :], riv[...], (((1,), (1,)), ((), ())),
                preferred_element_type=F32,
            ).astype(BF16)

    def keep(n, carry):
        contract(n, n)
        fetch_four(n).start()
        return carry

    def keep_fetched(n, carry):
        fetch_four(n).wait()
        contract(n, n + POOL // 4)
        return carry

    lax.fori_loop(0, 1, keep, 0)
    ro_ag = [ro_sum(0)]
    lax.fori_loop(1, 3, keep, 0)
    ro_ag.append(ro_sum(1))
    lax.fori_loop(3, 4, keep, 0)
    lax.fori_loop(0, 3, keep_fetched, 0)

    for c in range(2):
        for f in ro_ag[c]:
            f.wait_recv()
    rot[...] = rog[...].reshape(TOKENS, D_J).T.astype(F32)

    def score(q, p):
        sc[pl.ds(q, 1), :] = jnp.sum(p * rot[...], axis=0, keepdims=True)

    fetch_four(3).wait()

    def last(part, carry):
        p = lax.dot_general(
            pool[slot_rows(12 + part), :], riv[...], (((1,), (1,)), ((), ())), preferred_element_type=F32
        )
        for u in range(7):
            q = 7 * part + u
            score(q, pst[slot_rows(q), :].astype(F32))
        score(28 + part, p)
        return carry

    lax.fori_loop(0, 4, last, 0)

    parts = sc[...]
    high = parts.astype(BF16)
    rest = parts - high.astype(F32)
    middle = rest.astype(BF16)
    low_bits = (rest - middle.astype(F32)).astype(BF16)
    token = lax.broadcasted_iota(jnp.int32, (TOKENS, 128), 0)
    lane = lax.broadcasted_iota(jnp.int32, (TOKENS, 128), 1)
    pick = jnp.where(lane == lax.div(token, 16), 1.0, 0.0).astype(BF16)
    sums = jnp.dot(
        jnp.concatenate([high, middle, low_bits], axis=0), pick, preferred_element_type=F32
    )
    sums = sums[:32] + sums[32:64] + sums[64:]
    packed = sums[:8]
    for b in range(1, 4):
        packed = packed + pltpu.roll(sums[8 * b : 8 * b + 8], 16 * b, axis=1)
    ar_s[0] = packed
    c = send(ar_s.at[0], ar_r.at[0], AR_C, core_peer)
    c.wait_recv()
    packed = packed + ar_r[0]
    ar_s[1] = packed
    hops = [send(ar_s.at[1], ar_r.at[1 + n], AR_XY + n, xy_peer(d, e)) for n, (d, e) in enumerate(xy)]
    for c in hops:
        c.wait_recv()
    packed = packed + sum(ar_r[1 + n] for n in range(15))
    ar_s[2] = packed
    hops = [send(ar_s.at[2], ar_r.at[16 + d - 1], AR_Z + d - 1, z_peer(d)) for d in range(1, 8)]
    for c in hops:
        c.wait_recv()
    packed = packed + sum(ar_r[16 + n] for n in range(7))
    for b in range(4):
        out[8 * b : 8 * b + 8, :] = packed[:, 16 * b : 16 * b + 16]

    for c in started:
        c.wait_send()


def per_device(
    activations, out_grads, input_basis, output_basis, eigenvalues, query_inputs, query_outgrads
):
    any_, vmem = pl.BlockSpec(memory_space=pl.ANY), pl.BlockSpec(memory_space=pltpu.VMEM)
    piece = (16, WIDE // 2)
    scratch = [
        ((256, 256), BF16), ((256, D_I), BF16), ((512, D_I), BF16), ((512, D_J), BF16),
        ((2, 256, D_J), F32), ((D_J, D_I), F32), ((4, D_J, 128), BF16),
        ((POOL * D_J, D_I), BF16), ((28 * D_J, TOKENS), BF16),
        ((256, D_I), F32), ((128, D_I), F32), ((128, D_I), F32),
        ((2, 64, D_I), BF16), ((64, D_I), BF16), ((PARTS, 8, *piece), BF16), ((PARTS, 8, *piece), F32),
        ((PARTS, 8, *piece), BF16), ((2, PARTS, 2, 8, *piece), BF16), ((256, D_I), BF16),
        ((2, 8, HALF), F32), ((8, HALF), F32), ((2, 8, 2, 16, HALF), BF16),
        ((2, 8, 16, D_J), F32), ((2, 8, 16, D_J), BF16), ((2, 7, 16, D_J), BF16), ((16, 16, D_J), BF16),
        ((D_J, TOKENS), F32), ((QUERIES, TOKENS), F32), ((3, 8, 128), F32), ((23, 8, 128), F32),
    ]
    dma = pltpu.SemaphoreType.DMA
    scores, _ = pl.pallas_call(
        kernel,
        out_shape=[
            jax.ShapeDtypeStruct((QUERIES, SEQS), F32),
            jax.ShapeDtypeStruct(((QUERIES - POOL) * D_J, D_I), BF16),
        ],
        in_specs=[any_, any_, vmem, any_, any_, any_, any_],
        out_specs=[vmem, any_],
        scratch_shapes=[pltpu.VMEM(s, t) for s, t in scratch]
        + [dma((9,)), dma((16,)), dma((4,)), dma((N_SEMS,)), dma((N_SEMS,))],
        compiler_params=pltpu.CompilerParams(
            collective_id=0, has_side_effects=True, vmem_limit_bytes=63 * 2**20
        ),
        name="influence",
    )(activations, input_basis, out_grads, query_inputs, query_outgrads, eigenvalues, output_basis)
    return scores


def solution(mesh):
    in_specs = (
        P(None, "col"),
        P("col", "row"),
        P("col", "row"),
        P("row", "col"),
        P("row", "col"),
        P(None, "row"),
        P(None, "col"),
    )
    return jax.shard_map(
        per_device, mesh=mesh, in_specs=in_specs, out_specs=P(), check_vma=False
    )
```

```python
import functools

import jax
import jax.numpy as jnp
from jax import lax
from jax.experimental import pallas as pl
from jax.experimental.pallas import tpu as pltpu
from jax.sharding import PartitionSpec as P

MESH = pl.DeviceIdType.MESH
F32, BF16 = jnp.float32, jnp.bfloat16

D_I, D_J = 1024, 896
TOKENS, QUERIES, QTOK, SEQS = 256, 32, 16, 16
HALF = 1792
POOL = 16
PARTS = 2
WIDE = D_I // PARTS
DAMPING = 0.05
ORDER = (0, 1, 7, 2, 6, 3, 5, 4)

RI_CORE = 0
RI_X = RI_CORE + PARTS
RI_RS = RI_X + PARTS
RI_AG = RI_RS + 7 * PARTS
RI_AGX = RI_AG + 7 * PARTS
RI_AGC = RI_AGX + PARTS
OG_CORE = RI_AGC + PARTS
OG_Z = OG_CORE + 1
OG_X = OG_Z + 8
OG_C = OG_X + 8
RO_RS = OG_C + 16
RO_AG = RO_RS + 14
AR_C = RO_AG + 14
AR_XY = AR_C + 1
AR_Z = AR_XY + 15
N_SEMS = AR_Z + 7


def kernel(
    act, ib, og, qi, qo, eig, ob, out, spilled,
    act_v, ib_v, qi_v, qo_v, eig_v, wt, qa, pool, pst,
    rip, r1, acc1, s2, r2, s3, s3f, r3, rig, riv,
    ogx, ogr, ogg, rop, ros, ror, rog, rot, sc, ar_s, ar_r,
    lsem, osem, isem, ssem, rsem,
):
    row, col = lax.axis_index("row"), lax.axis_index("col")
    z, low = lax.div(col, 4), lax.rem(col, 4)
    xl, k = lax.div(low, 2), lax.rem(low, 2)
    core_peer = (row, col + 1 - 2 * k)
    x_col = z * 4 + lax.rem(low + 2, 4)
    x_peer = (row, x_col)

    def z_peer(d):
        return (row, lax.rem(z + d, 8) * 4 + low)

    def row_peer(d):
        return (lax.rem(row + d, 8), col)

    xy = [(d, e) for d in range(8) for e in range(2) if d or e]

    def xy_peer(d, e):
        return (lax.rem(row + d, 8), x_col if e else col)

    barrier = pltpu.get_barrier_semaphore()
    peers = [z_peer(d) for d in ORDER[:0:-1]] + [xy_peer(d, e) for d, e in xy] + [core_peer]
    for p in peers:
        pl.semaphore_signal(barrier, inc=1, device_id=p, device_id_type=MESH)

    started = []

    def send(src, dst, sem, peer):
        c = pltpu.make_async_remote_copy(
            src_ref=src, dst_ref=dst, send_sem=ssem.at[sem], recv_sem=rsem.at[sem],
            device_id=peer, device_id_type=MESH,
        )
        c.start()
        started.append(c)
        return c

    def fetch(src, dst, sem):
        c = pltpu.make_async_copy(src, dst, lsem.at[sem])
        c.start()
        return c

    ob_v = pool.at[pl.ds(0, 2 * HALF), pl.ds(0, D_J)]
    get_act = fetch(act, act_v, 0)
    get_ib = fetch(ib, ib_v, 1)
    get_eig = [fetch(eig.at[pl.ds(256 * c, 256)], eig_v.at[c % 2], 2 + c) for c in range(2)]
    get_qi = fetch(qi, qi_v, 6)
    get_qo = fetch(qo, qo_v, 7)

    own_og = og[...].astype(F32)
    ogx[0] = own_og[:, :HALF]
    ogx[1] = own_og[:, HALF:]

    get_act.wait()
    get_ib.wait()
    rip[...] = jnp.dot(act_v[...], ib_v[...], preferred_element_type=F32)

    pl.semaphore_wait(barrier, len(peers))

    def lanes(h):
        return pl.ds(WIDE * h, WIDE)

    og_c = send(ogx.at[1 - k], ogr, OG_CORE, core_peer)
    other_half = pl.ds(pl.multiple_of(128 - 128 * k, 128), 128)
    ri_c = [
        send(rip.at[other_half, lanes(h)], r1.at[:, lanes(h)], RI_CORE + h, core_peer)
        for h in range(PARTS)
    ]

    def slot_rows(slot, count=1):
        return pl.ds(pl.multiple_of(slot * D_J, D_J), count * D_J)

    def weighted(q, slot):
        group = lax.div(q, 8)
        tokens = qi_v[pl.ds(pl.multiple_of(group * 128, 128), 128), :]
        token = lax.broadcasted_iota(jnp.int32, tokens.shape, 0)
        own = jnp.where(lax.div(token, QTOK) == lax.rem(q, 8), tokens, jnp.zeros_like(tokens))
        for half in range(2):
            at = pl.ds(448 * half, 448)
            g = jnp.dot(qa[group, at, :], own, preferred_element_type=F32)
            rows = pl.ds(pl.multiple_of(slot * D_J + 448 * half, 448), 448)
            pool[rows, :] = (g.astype(BF16).astype(F32) * wt[at, :]).astype(BF16)

    def spill_copy(n, slot):
        return pltpu.make_async_copy(pool.at[slot_rows(slot), :], spilled.at[slot_rows(n), :], osem.at[n])

    def spill(n, carry):
        weighted(POOL + n, 4 + n)
        spill_copy(n, 4 + n).start()
        return carry

    def spill_last(n, carry):
        spill_copy(n - 12, n - 8).wait()
        weighted(POOL + n, n - 8)
        spill_copy(n, n - 8).start()
        return carry

    def fill_after_last(slot, carry):
        spill_copy(slot + 8, slot).wait()
        weighted(slot, slot)
        return carry

    def fill_after(slot, carry):
        spill_copy(slot - 4, slot).wait()
        weighted(slot, slot)
        return carry

    def fill(slot, carry):
        weighted(slot, slot)
        return carry

    ri_x = []
    for h in range(PARTS):
        ri_c[h].wait_recv()
        acc = rip[pl.ds(pl.multiple_of(128 * k, 128), 128), lanes(h)] + r1[:, lanes(h)]
        acc1[:, lanes(h)] = acc
        s2[0, :, lanes(h)] = acc[:64].astype(BF16)
        s2[1, :, lanes(h)] = acc[64:].astype(BF16)
        ri_x.append(send(s2.at[1 - xl, :, lanes(h)], r2.at[:, lanes(h)], RI_X + h, x_peer))

    og_c.wait_recv()
    mine = ogx[k]
    other = ogr[...]
    first = jnp.where(k == 0, mine, other)
    second = jnp.where(k == 0, other, mine)
    ogg[k, 0, xl] = jnp.concatenate([first, second], axis=0).astype(BF16)

    def og_send(n):
        return send(ogg.at[k, 0, xl], ogg.at[k, n, xl], OG_Z + n, z_peer(ORDER[n]))

    def og_pass(n, to, d):
        block = ogg.at[k, n, xl]
        og_z[to] = send(block, ogg.at[k, to, xl], OG_Z + to, z_peer(d))

    og_z = {n: og_send(n) for n in range(1, 5)}
    og_x, og_f = {}, {}

    def og_forward(n):
        if n:
            og_z[n].wait_recv()
        block = ogg.at[k, n, xl]
        if n not in (1, 2):
            og_x[n] = send(block, block, OG_X + n, x_peer)
        og_f[2 * n] = send(block, block, OG_C + 2 * n, core_peer)

    def og_forward_x(n):
        og_x[n].wait_recv()
        block = ogg.at[k, n, 1 - xl]
        og_f[2 * n + 1] = send(block, block, OG_C + 2 * n + 1, core_peer)
        if n == 0:
            for to, d in ((1, 1), (2, 7)):
                og_x[to] = send(block, ogg.at[k, to, 1 - xl], OG_X + to, z_peer(d))

    og_forward(0)
    for c in range(4):
        get_eig[c].wait()
        wt[:, pl.ds(256 * c, 256)] = 1.0 / (eig_v[c % 2].T + DAMPING)
        if c < 2:
            get_eig.append(fetch(eig.at[pl.ds(256 * (c + 2), 256)], eig_v.at[c % 2], 4 + c))
    get_ob = fetch(ob, ob_v, 8)
    get_qi.wait()
    get_qo.wait()
    for group in range(4):
        qa[group] = qo_v[128 * group : 128 * group + 128, :].T

    ri_rs = []
    for h in range(PARTS):
        ri_x[h].wait_recv()
        acc = acc1[pl.ds(pl.multiple_of(64 * xl, 64), 64), lanes(h)] + r2[:, lanes(h)].astype(F32)
        for c in range(8):
            at = WIDE // 2 * (c // 4)
            piece = acc[16 * (c % 4) : 16 * (c % 4) + 16, at : at + WIDE // 2]
            s3f[h, c] = piece
            s3[h, c] = piece.astype(BF16)
        ri_rs.append(
            [
                send(s3.at[h, lax.rem(z + d, 8)], r3.at[h, d], RI_RS + 7 * h + d - 1, z_peer(d))
                for d in ORDER[:0:-1]
            ]
        )
    og_forward_x(0)
    lax.fori_loop(0, 4, spill, 0, unroll=4)
    for n in range(3, 5):
        og_forward(n)
    og_pass(3, 5, 1)
    og_pass(4, 6, 7)
    og_pass(3, 7, 2)
    for n in range(1, 3):
        og_forward(n)

    lax.fori_loop(4, 12, spill, 0, unroll=4)
    for n in range(1, 4):
        og_forward_x(n)

    ri_ag = []
    for h in range(PARTS):
        for c in ri_rs[h]:
            c.wait_recv()
        total = s3f[h, z]
        for d in range(1, 8):
            total = total + r3[h, d].astype(F32)
        rig[k, h, xl, z] = total.astype(BF16)
        block = rig.at[k, h, xl, z]
        ri_ag.append([send(block, block, RI_AG + 7 * h + d - 1, z_peer(d)) for d in ORDER[:0:-1]])

    lax.fori_loop(12, 16, spill_last, 0, unroll=4)
    for n in range(5, 8):
        og_forward(n)
    og_forward_x(4)
    lax.fori_loop(8, 12, fill_after, 0, unroll=4)

    def ro_start(c):
        for n in range(8 * c, 8 * c + 8):
            og_f[n].wait_recv()
        tokens = [ogg[a, 4 * c : 4 * c + 4].reshape(128, HALF) for a in range(2)]
        part = jnp.dot(tokens[0], pool[pl.ds(0, HALF), pl.ds(0, D_J)], preferred_element_type=F32)
        part = part + jnp.dot(
            tokens[1], pool[pl.ds(HALF, HALF), pl.ds(0, D_J)], preferred_element_type=F32
        )
        rop[c] = part.reshape(8, 16, D_J)
        ros[c] = part.reshape(8, 16, D_J).astype(BF16)
        return [
            send(ros.at[c, lax.rem(row + d, 8)], ror.at[c, d - 1], RO_RS + 7 * c + d - 1, row_peer(d))
            for d in range(1, 8)
        ]

    def ro_sum(c):
        for f in ro_rs[c]:
            f.wait_recv()
        total = rop[c, row]
        for d in range(1, 8):
            total = total + ror[c, d - 1].astype(F32)
        n = 4 * c + lax.div(row, 2)
        far = lax.div(n + 1, 2)
        source = lax.rem(jnp.where(lax.rem(n, 2) == 1, z + 8 - far, z + far), 8)
        seq = 2 * source + lax.rem(row, 2)
        rog[seq] = total.astype(BF16)
        block = rog.at[seq]
        return [send(block, block, RO_AG + 7 * c + d - 1, row_peer(d)) for d in range(1, 8)]

    get_ob.wait()
    ro_rs = [ro_start(0)]

    ri_agx = []
    for h in range(PARTS):
        for c in ri_ag[h]:
            c.wait_recv()
        block = rig.at[k, h, xl]
        ri_agx.append(send(block, block, RI_AGX + h, x_peer))

    lax.fori_loop(12, 16, fill_after, 0, unroll=4)
    for n in range(5, 8):
        og_forward_x(n)
    ro_rs.append(ro_start(1))
    lax.fori_loop(4, 8, fill_after_last, 0, unroll=4)
    ri_agc = []
    for h in range(PARTS):
        ri_agx[h].wait_recv()
        ri_agc.append(send(rig.at[k, h], rig.at[k, h], RI_AGC + h, core_peer))
    lax.fori_loop(0, 4, fill, 0, unroll=4)

    for h in range(PARTS):
        ri_agc[h].wait_recv()
        for a in range(2):
            for b in range(2):
                for c in range(8):
                    at = 128 * a + 64 * b + 16 * (c % 4)
                    lane = WIDE * h + WIDE // 2 * (c // 4)
                    riv[at : at + 16, lane : lane + WIDE // 2] = rig[a, h, b, c]

    def fetch_four(n):
        rows = slot_rows(4 * n, 4)
        return pltpu.make_async_copy(spilled.at[rows, :], pool.at[rows, :], isem.at[n])

    def contract(n, to):
        for part in range(4):
            pst[slot_rows(4 * to + part), :] = lax.dot_general(
                pool[slot_rows(4 * n + part), :], riv[...], (((1,), (1,)), ((), ())),
                preferred_element_type=F32,
            ).astype(BF16)

    def keep(n, carry):
        contract(n, n)
        fetch_four(n).start()
        return carry

    def keep_fetched(n, carry):
        fetch_four(n).wait()
        contract(n, n + POOL // 4)
        return carry

    lax.fori_loop(0, 1, keep, 0)
    ro_ag = [ro_sum(0)]
    lax.fori_loop(1, 2, keep, 0)
    ro_ag.append(ro_sum(1))
    lax.fori_loop(2, 4, keep, 0)
    lax.fori_loop(0, 2, keep_fetched, 0)

    for c in range(2):
        for f in ro_ag[c]:
            f.wait_recv()
    rot[...] = rog[...].reshape(TOKENS, D_J).T.astype(F32)

    def score(q, p):
        sc[pl.ds(q, 1), :] = jnp.sum(p * rot[...], axis=0, keepdims=True)

    fetch_four(2).wait()
    fetch_four(3).wait()

    def last(part, carry):
        p = lax.dot_general(
            pool[slot_rows(8 + part), :], riv[...], (((1,), (1,)), ((), ())), preferred_element_type=F32
        )
        for u in range(3):
            q = 3 * part + u
            score(q, pst[slot_rows(q), :].astype(F32))
        score(24 + part, p)
        return carry

    lax.fori_loop(0, 8, last, 0, unroll=2)

    parts = sc[...]
    high = parts.astype(BF16)
    rest = parts - high.astype(F32)
    middle = rest.astype(BF16)
    low_bits = (rest - middle.astype(F32)).astype(BF16)
    token = lax.broadcasted_iota(jnp.int32, (TOKENS, 128), 0)
    lane = lax.broadcasted_iota(jnp.int32, (TOKENS, 128), 1)
    pick = jnp.where(lane == lax.div(token, 16), 1.0, 0.0).astype(BF16)
    sums = jnp.dot(
        jnp.concatenate([high, middle, low_bits], axis=0), pick, preferred_element_type=F32
    )
    sums = sums[:32] + sums[32:64] + sums[64:]
    packed = sums[:8]
    for b in range(1, 4):
        packed = packed + pltpu.roll(sums[8 * b : 8 * b + 8], 16 * b, axis=1)
    ar_s[0] = packed
    c = send(ar_s.at[0], ar_r.at[0], AR_C, core_peer)
    c.wait_recv()
    packed = packed + ar_r[0]
    ar_s[1] = packed
    earlier = list(started)
    started.clear()
    hops = [send(ar_s.at[1], ar_r.at[1 + n], AR_XY + n, xy_peer(d, e)) for n, (d, e) in enumerate(xy)]
    for c in earlier:
        c.wait_send()
    for c in hops:
        c.wait_recv()
    packed = packed + sum(ar_r[1 + n] for n in range(15))
    ar_s[2] = packed
    hops = [send(ar_s.at[2], ar_r.at[16 + d - 1], AR_Z + d - 1, z_peer(d)) for d in range(1, 8)]
    for c in hops:
        c.wait_recv()
    packed = packed + sum(ar_r[16 + n] for n in range(7))
    for b in range(4):
        out[8 * b : 8 * b + 8, :] = packed[:, 16 * b : 16 * b + 16]

    for c in started:
        c.wait_send()


def per_device(
    activations, out_grads, input_basis, output_basis, eigenvalues, query_inputs, query_outgrads
):
    any_, vmem = pl.BlockSpec(memory_space=pl.ANY), pl.BlockSpec(memory_space=pltpu.VMEM)
    piece = (16, WIDE // 2)
    scratch = [
        ((256, 256), BF16), ((256, D_I), BF16), ((512, D_I), BF16), ((512, D_J), BF16),
        ((2, 256, D_J), F32), ((D_J, D_I), F32), ((4, D_J, 128), BF16),
        ((POOL * D_J, D_I), BF16), ((24 * D_J, TOKENS), BF16),
        ((256, D_I), F32), ((128, D_I), F32), ((128, D_I), F32),
        ((2, 64, D_I), BF16), ((64, D_I), BF16), ((PARTS, 8, *piece), BF16), ((PARTS, 8, *piece), F32),
        ((PARTS, 8, *piece), BF16), ((2, PARTS, 2, 8, *piece), BF16), ((256, D_I), BF16),
        ((2, 8, HALF), F32), ((8, HALF), F32), ((2, 8, 2, 16, HALF), BF16),
        ((2, 8, 16, D_J), F32), ((2, 8, 16, D_J), BF16), ((2, 7, 16, D_J), BF16), ((16, 16, D_J), BF16),
        ((D_J, TOKENS), F32), ((QUERIES, TOKENS), F32), ((3, 8, 128), F32), ((23, 8, 128), F32),
    ]
    dma = pltpu.SemaphoreType.DMA
    scores, _ = pl.pallas_call(
        kernel,
        out_shape=[
            jax.ShapeDtypeStruct((QUERIES, SEQS), F32),
            jax.ShapeDtypeStruct(((QUERIES - POOL) * D_J, D_I), BF16),
        ],
        in_specs=[any_, any_, vmem, any_, any_, any_, any_],
        out_specs=[vmem, any_],
        scratch_shapes=[pltpu.VMEM(s, t) for s, t in scratch]
        + [dma((9,)), dma((16,)), dma((4,)), dma((N_SEMS,)), dma((N_SEMS,))],
        compiler_params=pltpu.CompilerParams(
            collective_id=0, has_side_effects=True, vmem_limit_bytes=63 * 2**20
        ),
        name="influence",
    )(activations, input_basis, out_grads, query_inputs, query_outgrads, eigenvalues, output_basis)
    return scores


def solution(mesh):
    in_specs = (
        P(None, "col"),
        P("col", "row"),
        P("col", "row"),
        P("row", "col"),
        P("row", "col"),
        P(None, "row"),
        P(None, "col"),
    )
    return jax.shard_map(
        per_device, mesh=mesh, in_specs=in_specs, out_specs=P(), check_vma=False
    )
```

```python
import functools

import jax
import jax.numpy as jnp
from jax import lax
from jax.experimental import pallas as pl
from jax.experimental.pallas import tpu as pltpu
from jax.sharding import PartitionSpec as P

MESH = pl.DeviceIdType.MESH
F32, BF16 = jnp.float32, jnp.bfloat16

D_I, D_J = 1024, 896
TOKENS, QUERIES, QTOK, SEQS = 256, 32, 16, 16
HALF = 1792
POOL = 16
PARTS = 2
WIDE = D_I // PARTS
DAMPING = 0.05
ORDER = (0, 1, 7, 2, 6, 3, 5, 4)

RI_CORE = 0
RI_X = RI_CORE + PARTS
RI_RS = RI_X + PARTS
RI_AG = RI_RS + 7 * PARTS
RI_AGX = RI_AG + 7 * PARTS
RI_AGC = RI_AGX + PARTS
OG_CORE = RI_AGC + PARTS
OG_Z = OG_CORE + 1
OG_X = OG_Z + 8
OG_C = OG_X + 8
RO_RS = OG_C + 16
RO_AG = RO_RS + 14
AR_C = RO_AG + 14
AR_XY = AR_C + 1
AR_Z = AR_XY + 15
N_SEMS = AR_Z + 7


def kernel(
    act, ib, og, qi, qo, eig, ob, out, spilled,
    act_v, ib_v, qi_v, qo_v, eig_v, wt, qa, pool, pst,
    rip, r1, acc1, s2, r2, s3, s3f, r3, rig, riv,
    ogx, ogr, ogg, rop, ros, ror, rog, rot, sc, ar_s, ar_r,
    lsem, osem, isem, ssem, rsem,
):
    row, col = lax.axis_index("row"), lax.axis_index("col")
    z, low = lax.div(col, 4), lax.rem(col, 4)
    xl, k = lax.div(low, 2), lax.rem(low, 2)
    core_peer = (row, col + 1 - 2 * k)
    x_col = z * 4 + lax.rem(low + 2, 4)
    x_peer = (row, x_col)

    def z_peer(d):
        return (row, lax.rem(z + d, 8) * 4 + low)

    def row_peer(d):
        return (lax.rem(row + d, 8), col)

    xy = [(d, e) for d in range(8) for e in range(2) if d or e]

    def xy_peer(d, e):
        return (lax.rem(row + d, 8), x_col if e else col)

    barrier = pltpu.get_barrier_semaphore()
    peers = [z_peer(d) for d in ORDER[:0:-1]] + [xy_peer(d, e) for d, e in xy] + [core_peer]
    for p in peers:
        pl.semaphore_signal(barrier, inc=1, device_id=p, device_id_type=MESH)

    started = []

    def send(src, dst, sem, peer):
        c = pltpu.make_async_remote_copy(
            src_ref=src, dst_ref=dst, send_sem=ssem.at[sem], recv_sem=rsem.at[sem],
            device_id=peer, device_id_type=MESH,
        )
        c.start()
        started.append(c)
        return c

    def fetch(src, dst, sem):
        c = pltpu.make_async_copy(src, dst, lsem.at[sem])
        c.start()
        return c

    ob_v = pool.at[pl.ds(0, 2 * HALF), pl.ds(0, D_J)]
    get_act = fetch(act, act_v, 0)
    get_ib = fetch(ib, ib_v, 1)
    get_eig = [fetch(eig.at[pl.ds(256 * c, 256)], eig_v.at[c % 2], 2 + c) for c in range(2)]
    get_qi = fetch(qi, qi_v, 6)
    get_qo = fetch(qo, qo_v, 7)

    own_og = og[...].astype(F32)
    ogx[0] = own_og[:, :HALF]
    ogx[1] = own_og[:, HALF:]

    get_act.wait()
    get_ib.wait()
    rip[...] = jnp.dot(act_v[...], ib_v[...], preferred_element_type=F32)

    pl.semaphore_wait(barrier, len(peers))

    def lanes(h):
        return pl.ds(WIDE * h, WIDE)

    og_c = send(ogx.at[1 - k], ogr, OG_CORE, core_peer)
    other_half = pl.ds(pl.multiple_of(128 - 128 * k, 128), 128)
    ri_c = [
        send(rip.at[other_half, lanes(h)], r1.at[:, lanes(h)], RI_CORE + h, core_peer)
        for h in range(PARTS)
    ]

    def slot_rows(slot, count=1):
        return pl.ds(pl.multiple_of(slot * D_J, D_J), count * D_J)

    def weighted(q, slot):
        group = lax.div(q, 8)
        tokens = qi_v[pl.ds(pl.multiple_of(group * 128, 128), 128), :]
        token = lax.broadcasted_iota(jnp.int32, tokens.shape, 0)
        own = jnp.where(lax.div(token, QTOK) == lax.rem(q, 8), tokens, jnp.zeros_like(tokens))
        for half in range(2):
            at = pl.ds(448 * half, 448)
            g = jnp.dot(qa[group, at, :], own, preferred_element_type=F32)
            rows = pl.ds(pl.multiple_of(slot * D_J + 448 * half, 448), 448)
            pool[rows, :] = (g.astype(BF16).astype(F32) * wt[at, :]).astype(BF16)

    def spill_copy(n, slot):
        return pltpu.make_async_copy(pool.at[slot_rows(slot), :], spilled.at[slot_rows(n), :], osem.at[n])

    def spill(n, carry):
        weighted(POOL + n, 4 + n)
        spill_copy(n, 4 + n).start()
        return carry

    def spill_last(n, carry):
        spill_copy(n - 12, n - 8).wait()
        weighted(POOL + n, n - 8)
        spill_copy(n, n - 8).start()
        return carry

    def fill_after_last(slot, carry):
        spill_copy(slot + 8, slot).wait()
        weighted(slot, slot)
        return carry

    def fill_after(slot, carry):
        spill_copy(slot - 4, slot).wait()
        weighted(slot, slot)
        return carry

    def fill(slot, carry):
        weighted(slot, slot)
        return carry

    def invert(begin, end):
        for c in range(begin, end):
            get_eig[c].wait()
            wt[:, pl.ds(256 * c, 256)] = 1.0 / (eig_v[c % 2].T + DAMPING)
            if c < 2:
                get_eig.append(fetch(eig.at[pl.ds(256 * (c + 2), 256)], eig_v.at[c % 2], 4 + c))

    invert(0, 2)
    ri_x = []
    for h in range(PARTS):
        ri_c[h].wait_recv()
        acc = rip[pl.ds(pl.multiple_of(128 * k, 128), 128), lanes(h)] + r1[:, lanes(h)]
        acc1[:, lanes(h)] = acc
        s2[0, :, lanes(h)] = acc[:64].astype(BF16)
        s2[1, :, lanes(h)] = acc[64:].astype(BF16)
        ri_x.append(send(s2.at[1 - xl, :, lanes(h)], r2.at[:, lanes(h)], RI_X + h, x_peer))

    og_c.wait_recv()
    mine = ogx[k]
    other = ogr[...]
    first = jnp.where(k == 0, mine, other)
    second = jnp.where(k == 0, other, mine)
    ogg[k, 0, xl] = jnp.concatenate([first, second], axis=0).astype(BF16)

    def og_send(n):
        return send(ogg.at[k, 0, xl], ogg.at[k, n, xl], OG_Z + n, z_peer(ORDER[n]))

    def og_pass(n, to, d):
        block = ogg.at[k, n, xl]
        og_z[to] = send(block, ogg.at[k, to, xl], OG_Z + to, z_peer(d))

    og_z = {n: og_send(n) for n in range(1, 5)}
    og_x, og_f = {}, {}

    def og_forward(n):
        if n:
            og_z[n].wait_recv()
        block = ogg.at[k, n, xl]
        if n not in (1, 2):
            og_x[n] = send(block, block, OG_X + n, x_peer)
        og_f[2 * n] = send(block, block, OG_C + 2 * n, core_peer)

    def og_forward_x(n):
        og_x[n].wait_recv()
        block = ogg.at[k, n, 1 - xl]
        og_f[2 * n + 1] = send(block, block, OG_C + 2 * n + 1, core_peer)
        if n == 0:
            for to, d in ((1, 1), (2, 7)):
                og_x[to] = send(block, ogg.at[k, to, 1 - xl], OG_X + to, z_peer(d))

    og_forward(0)
    invert(2, 4)
    get_ob = fetch(ob, ob_v, 8)
    get_qi.wait()
    get_qo.wait()
    for group in range(4):
        qa[group] = qo_v[128 * group : 128 * group + 128, :].T

    ri_rs = []
    for h in range(PARTS):
        ri_x[h].wait_recv()
        acc = acc1[pl.ds(pl.multiple_of(64 * xl, 64), 64), lanes(h)] + r2[:, lanes(h)].astype(F32)
        for c in range(8):
            at = WIDE // 2 * (c // 4)
            piece = acc[16 * (c % 4) : 16 * (c % 4) + 16, at : at + WIDE // 2]
            s3f[h, c] = piece
            s3[h, c] = piece.astype(BF16)
        ri_rs.append(
            [
                send(s3.at[h, lax.rem(z + d, 8)], r3.at[h, d], RI_RS + 7 * h + d - 1, z_peer(d))
                for d in ORDER[:0:-1]
            ]
        )
    og_forward_x(0)
    lax.fori_loop(0, 4, spill, 0, unroll=4)
    for n in range(3, 5):
        og_forward(n)
    og_pass(3, 5, 1)
    og_pass(4, 6, 7)
    og_pass(3, 7, 2)
    for n in range(1, 3):
        og_forward(n)

    lax.fori_loop(4, 12, spill, 0, unroll=4)
    for n in range(1, 4):
        og_forward_x(n)

    ri_ag = []
    for h in range(PARTS):
        for c in ri_rs[h]:
            c.wait_recv()
        total = s3f[h, z]
        for d in range(1, 8):
            total = total + r3[h, d].astype(F32)
        rig[k, h, xl, z] = total.astype(BF16)
        block = rig.at[k, h, xl, z]
        ri_ag.append([send(block, block, RI_AG + 7 * h + d - 1, z_peer(d)) for d in ORDER[:0:-1]])

    lax.fori_loop(12, 16, spill_last, 0, unroll=4)
    for n in range(5, 8):
        og_forward(n)
    og_forward_x(4)
    lax.fori_loop(8, 12, fill_after, 0, unroll=4)

    def ro_start(c):
        for n in range(8 * c, 8 * c + 8):
            og_f[n].wait_recv()
        tokens = [ogg[a, 4 * c : 4 * c + 4].reshape(128, HALF) for a in range(2)]
        part = jnp.dot(tokens[0], pool[pl.ds(0, HALF), pl.ds(0, D_J)], preferred_element_type=F32)
        part = part + jnp.dot(
            tokens[1], pool[pl.ds(HALF, HALF), pl.ds(0, D_J)], preferred_element_type=F32
        )
        rop[c] = part.reshape(8, 16, D_J)
        ros[c] = part.reshape(8, 16, D_J).astype(BF16)
        return [
            send(ros.at[c, lax.rem(row + d, 8)], ror.at[c, d - 1], RO_RS + 7 * c + d - 1, row_peer(d))
            for d in range(1, 8)
        ]

    def ro_sum(c):
        for f in ro_rs[c]:
            f.wait_recv()
        total = rop[c, row]
        for d in range(1, 8):
            total = total + ror[c, d - 1].astype(F32)
        n = 4 * c + lax.div(row, 2)
        far = lax.div(n + 1, 2)
        source = lax.rem(jnp.where(lax.rem(n, 2) == 1, z + 8 - far, z + far), 8)
        seq = 2 * source + lax.rem(row, 2)
        rog[seq] = total.astype(BF16)
        block = rog.at[seq]
        return [send(block, block, RO_AG + 7 * c + d - 1, row_peer(d)) for d in range(1, 8)]

    get_ob.wait()
    ro_rs = [ro_start(0)]

    ri_agx = []
    for h in range(PARTS):
        for c in ri_ag[h]:
            c.wait_recv()
        block = rig.at[k, h, xl]
        ri_agx.append(send(block, block, RI_AGX + h, x_peer))

    lax.fori_loop(12, 16, fill_after, 0, unroll=4)
    for n in range(5, 8):
        og_forward_x(n)
    ro_rs.append(ro_start(1))
    lax.fori_loop(4, 8, fill_after_last, 0, unroll=4)
    ri_agc = []
    for h in range(PARTS):
        ri_agx[h].wait_recv()
        ri_agc.append(send(rig.at[k, h], rig.at[k, h], RI_AGC + h, core_peer))
    lax.fori_loop(0, 4, fill, 0, unroll=4)

    for h in range(PARTS):
        ri_agc[h].wait_recv()
        for a in range(2):
            for b in range(2):
                for c in range(8):
                    at = 128 * a + 64 * b + 16 * (c % 4)
                    lane = WIDE * h + WIDE // 2 * (c // 4)
                    riv[at : at + 16, lane : lane + WIDE // 2] = rig[a, h, b, c]

    def fetch_four(n):
        rows = slot_rows(4 * n, 4)
        return pltpu.make_async_copy(spilled.at[rows, :], pool.at[rows, :], isem.at[n])

    def contract(n, to):
        for part in range(4):
            pst[slot_rows(4 * to + part), :] = lax.dot_general(
                pool[slot_rows(4 * n + part), :], riv[...], (((1,), (1,)), ((), ())),
                preferred_element_type=F32,
            ).astype(BF16)

    def keep(n, carry):
        contract(n, n)
        fetch_four(n).start()
        return carry

    def keep_fetched(n, carry):
        fetch_four(n).wait()
        contract(n, n + POOL // 4)
        return carry

    lax.fori_loop(0, 1, keep, 0)
    ro_ag = [ro_sum(0)]
    lax.fori_loop(1, 2, keep, 0)
    ro_ag.append(ro_sum(1))
    lax.fori_loop(2, 4, keep, 0)
    lax.fori_loop(0, 2, keep_fetched, 0)

    for c in range(2):
        for f in ro_ag[c]:
            f.wait_recv()
    rot[...] = rog[...].reshape(TOKENS, D_J).T.astype(F32)

    def score(q, p):
        sc[pl.ds(q, 1), :] = jnp.sum(p * rot[...], axis=0, keepdims=True)

    fetch_four(2).wait()
    fetch_four(3).wait()

    def last(part, carry):
        p = lax.dot_general(
            pool[slot_rows(8 + part), :], riv[...], (((1,), (1,)), ((), ())), preferred_element_type=F32
        )
        for u in range(3):
            q = 3 * part + u
            score(q, pst[slot_rows(q), :].astype(F32))
        score(24 + part, p)
        return carry

    lax.fori_loop(0, 8, last, 0, unroll=2)

    parts = sc[...]
    high = parts.astype(BF16)
    rest = parts - high.astype(F32)
    middle = rest.astype(BF16)
    low_bits = (rest - middle.astype(F32)).astype(BF16)
    token = lax.broadcasted_iota(jnp.int32, (TOKENS, 128), 0)
    lane = lax.broadcasted_iota(jnp.int32, (TOKENS, 128), 1)
    pick = jnp.where(lane == lax.div(token, 16), 1.0, 0.0).astype(BF16)
    sums = jnp.dot(
        jnp.concatenate([high, middle, low_bits], axis=0), pick, preferred_element_type=F32
    )
    sums = sums[:32] + sums[32:64] + sums[64:]
    packed = sums[:8]
    for b in range(1, 4):
        packed = packed + pltpu.roll(sums[8 * b : 8 * b + 8], 16 * b, axis=1)
    ar_s[0] = packed
    c = send(ar_s.at[0], ar_r.at[0], AR_C, core_peer)
    c.wait_recv()
    packed = packed + ar_r[0]
    ar_s[1] = packed
    earlier = list(started)
    started.clear()
    hops = [send(ar_s.at[1], ar_r.at[1 + n], AR_XY + n, xy_peer(d, e)) for n, (d, e) in enumerate(xy)]
    for c in earlier:
        c.wait_send()
    for c in hops:
        c.wait_recv()
    packed = packed + sum(ar_r[1 + n] for n in range(15))
    ar_s[2] = packed
    hops = [send(ar_s.at[2], ar_r.at[16 + d - 1], AR_Z + d - 1, z_peer(d)) for d in range(1, 8)]
    for c in hops:
        c.wait_recv()
    packed = packed + sum(ar_r[16 + n] for n in range(7))
    for b in range(4):
        out[8 * b : 8 * b + 8, :] = packed[:, 16 * b : 16 * b + 16]

    for c in started:
        c.wait_send()


def per_device(
    activations, out_grads, input_basis, output_basis, eigenvalues, query_inputs, query_outgrads
):
    any_, vmem = pl.BlockSpec(memory_space=pl.ANY), pl.BlockSpec(memory_space=pltpu.VMEM)
    piece = (16, WIDE // 2)
    scratch = [
        ((256, 256), BF16), ((256, D_I), BF16), ((512, D_I), BF16), ((512, D_J), BF16),
        ((2, 256, D_J), F32), ((D_J, D_I), F32), ((4, D_J, 128), BF16),
        ((POOL * D_J, D_I), BF16), ((24 * D_J, TOKENS), BF16),
        ((256, D_I), F32), ((128, D_I), F32), ((128, D_I), F32),
        ((2, 64, D_I), BF16), ((64, D_I), BF16), ((PARTS, 8, *piece), BF16), ((PARTS, 8, *piece), F32),
        ((PARTS, 8, *piece), BF16), ((2, PARTS, 2, 8, *piece), BF16), ((256, D_I), BF16),
        ((2, 8, HALF), F32), ((8, HALF), F32), ((2, 8, 2, 16, HALF), BF16),
        ((2, 8, 16, D_J), F32), ((2, 8, 16, D_J), BF16), ((2, 7, 16, D_J), BF16), ((16, 16, D_J), BF16),
        ((D_J, TOKENS), F32), ((QUERIES, TOKENS), F32), ((3, 8, 128), F32), ((23, 8, 128), F32),
    ]
    dma = pltpu.SemaphoreType.DMA
    scores, _ = pl.pallas_call(
        kernel,
        out_shape=[
            jax.ShapeDtypeStruct((QUERIES, SEQS), F32),
            jax.ShapeDtypeStruct(((QUERIES - POOL) * D_J, D_I), BF16),
        ],
        in_specs=[any_, any_, vmem, any_, any_, any_, any_],
        out_specs=[vmem, any_],
        scratch_shapes=[pltpu.VMEM(s, t) for s, t in scratch]
        + [dma((9,)), dma((16,)), dma((4,)), dma((N_SEMS,)), dma((N_SEMS,))],
        compiler_params=pltpu.CompilerParams(
            collective_id=0, has_side_effects=True, vmem_limit_bytes=63 * 2**20
        ),
        name="influence",
    )(activations, input_basis, out_grads, query_inputs, query_outgrads, eigenvalues, output_basis)
    return scores


def solution(mesh):
    in_specs = (
        P(None, "col"),
        P("col", "row"),
        P("col", "row"),
        P("row", "col"),
        P("row", "col"),
        P(None, "row"),
        P(None, "col"),
    )
    return jax.shard_map(
        per_device, mesh=mesh, in_specs=in_specs, out_specs=P(), check_vma=False
    )
```
